512 devices in a mesh: attn: 16 (over x, z_lo), ffn: 4 (over z_hi), tp: 8 (over y, core).
Axes of the slice: x: 4, y: 4, z: 16 (z_hi: 4, z_lo: 4; z = z_hi * 4 + z_lo), core: 2. Of those that a mesh axis runs over, the one named last changes fastest.
Arguments:
- x_init: bfloat16 [192, 8192], P(('attn', 'ffn'), 'tp'), may hold values from -14 to 14
- queries: bfloat16 [3, 192, 64, 128], P(None, ('attn', 'ffn'), 'tp'), may hold values from -120 to 120
- new_kv: bfloat16 [3, 192, 8, 2, 128], P(None, ('attn', 'ffn'), 'tp'), may hold values from -6 to 6
- kv_cache: bfloat16 [192, 8, 2, 1024, 128], P(('attn', 'ffn'), 'tp'), may hold values from -6 to 6
- lengths: int32 [192], P(('attn', 'ffn')), may hold values from 2 to 1024, as said below
- norm_gain: bfloat16 [8192], P('tp'), may hold values from 0.099609375 to 1.8984375
- w_gate_up: bfloat16 [8192, 2, 32768], P('tp', None, ('attn', 'ffn')), may hold values from -0.0625 to 0.0625
- w_down: bfloat16 [32768, 8192], P(('attn', 'ffn'), 'tp'), may hold values from -0.03125 to 0.03125
Outputs:
- outputs: bfloat16 [3, 192, 8192], P(None, ('attn', 'ffn'), 'tp')
The draws below stay inside these ranges and needn't reach their ends.
Inputs may be any that keep to these rules, and one draw needn't show every extreme that they name: `lengths`: every request has 2 or more live positions; the largest length is exactly 1024.
All inputs are finite; a program needn't handle non-finite values.
Results may differ from the reference program's by a relative error of at most 0.024.
Values may be sent and summed in bfloat16 or wider, within the bound.
No kernel may reach another device: no remote copies, remote signals or barrier semaphores. Data moves between devices by JAX's collectives and lax.ppermute only.
A program may use at most 64 MiB of HBM per device.

```python
import jax
import jax.numpy as jnp
from jax import lax

HEADS = 64
KVH = 8
HD = 128
D = 8192
FF = 32768
R_DEV = 3
LMAX = 1024
STEPS = 3
BATCH = 192
N_TP = 8


def cache_base(key):
    return jnp.clip(jax.random.normal(key, (BATCH, KVH, LMAX, HD), jnp.float32), -6.0, 6.0)


def draw_kv_cache(key, part):
    cache_keys = cache_base(key)
    key = jax.random.fold_in(key, 3)
    cache_values = jnp.clip(jax.random.normal(key, (BATCH, KVH, LMAX, HD), jnp.float32), -6.0, 6.0)
    return jnp.stack([cache_keys, cache_values], axis=2).astype(jnp.bfloat16)


def draw_queries(key, part):
    key = jax.random.fold_in(key, 5)
    first_key = jax.random.fold_in(key, 0)
    drawn = jnp.clip(jax.random.normal(first_key, (STEPS, BATCH, HEADS, HD), jnp.float32), -6.0, 6.0)
    return drawn.astype(jnp.bfloat16)


def draw_x_init(key, part):
    key = jax.random.fold_in(key, 7)
    base_values = jnp.clip(jax.random.normal(key, (BATCH, D), jnp.float32), -5.0, 5.0)
    column_pos = jnp.arange(D, dtype=jnp.float32) / D
    column_scale = 0.5 * 3.0 ** column_pos
    return (base_values * column_scale[None, :]).astype(jnp.bfloat16)


def draw_lengths(key, part):
    key = jax.random.fold_in(key, 9)
    first_key, second_key, third_key = jax.random.split(key, 3)
    levels = jax.random.randint(first_key, (BATCH // R_DEV,), 1, 5)
    upper = 2 + (LMAX - 2) * levels // 4
    row_upper = jnp.repeat(upper, R_DEV)
    drawn = jax.random.randint(second_key, (BATCH,), 2, row_upper + 1)
    chosen = jax.random.randint(third_key, (), 0, BATCH)
    return jnp.where(jnp.arange(BATCH) == chosen, LMAX, drawn).astype(jnp.int32)


def shard_levels(stream_key, extent, pieces, least, top_value):
    factor_of = 1.0
    for position, parts in pieces:
        steps = jax.random.uniform(jax.random.fold_in(jax.random.fold_in(stream_key, 6), position), (parts,), jnp.float32, least / len(pieces), top_value / len(pieces))
        factor_of = factor_of * jnp.repeat(jnp.exp(steps), extent[position] // parts).reshape((-1,) + (1,) * (len(extent) - 1 - position))
    return factor_of


def gaussian(rng, dims, scale, limit, pieces=(), held_as=jnp.bfloat16):
    factor_of = shard_levels(rng, dims, pieces, -0.22, 0.18) if pieces else 1.0
    entries = jax.random.normal(rng, dims, jnp.float32) * scale * factor_of
    return jnp.minimum(jnp.maximum(entries, -limit), limit).astype(held_as)


def setup_inputs(seed: int = 0) -> dict:
    streams_of = jax.random.split(jax.random.key(seed), 9)
    return {
        "x_init": draw_x_init(jax.random.fold_in(streams_of[8], 71), 0),
        "queries": draw_queries(jax.random.fold_in(streams_of[8], 71), 0),
        "new_kv": gaussian(streams_of[2], (STEPS, BATCH, KVH, 2, HD), 1.0, 6.0, ((1, 64), (2, 8))),
        "kv_cache": draw_kv_cache(jax.random.fold_in(streams_of[8], 71), 0),
        "lengths": draw_lengths(jax.random.fold_in(streams_of[8], 71), 0),
        "norm_gain": jnp.clip(1.0 + 0.18 * jax.random.normal(streams_of[5], (D,), jnp.float32), 0.099609375, 1.8984375).astype(jnp.bfloat16),
        "w_gate_up": gaussian(streams_of[6], (D, 2, FF), D ** -0.5, 0.0625, ((0, 8), (2, 64))),
        "w_down": gaussian(streams_of[7], (FF, D), FF ** -0.5, 0.03125, ((0, 64), (1, 8))),
    }


def attend_one(query_rows, cache_block, fresh_keys, fresh_values, live_length):
    group_size = HEADS // KVH
    score_scale = HD ** (-0.5)
    grouped = query_rows.astype(jnp.float32).reshape(KVH, group_size, HD)
    cache_keys = cache_block[:, 0].astype(jnp.float32)
    cache_values = cache_block[:, 1].astype(jnp.float32)
    cache_scores = jnp.einsum('kgd,kld->kgl', grouped, cache_keys) * score_scale
    live_mask = jnp.arange(LMAX, dtype=jnp.int32) < live_length
    cache_scores = jnp.where(live_mask[None, None, :], cache_scores, -1e+30)
    fresh_scores = jnp.einsum('kgd,nkd->kgn', grouped, fresh_keys.astype(jnp.float32)) * score_scale
    row_max = jnp.maximum(lax.optimization_barrier(jnp.max(cache_scores, axis=-1)), lax.optimization_barrier(jnp.max(fresh_scores, axis=-1)))[..., None]
    cache_exp = jnp.exp(cache_scores - row_max)
    fresh_exp = jnp.exp(fresh_scores - row_max)
    exp_total = lax.optimization_barrier(jnp.sum(cache_exp, axis=-1, keepdims=True)) + lax.optimization_barrier(jnp.sum(fresh_exp, axis=-1, keepdims=True))
    cache_probs = (cache_exp / exp_total).astype(jnp.bfloat16)
    fresh_probs = (fresh_exp / exp_total).astype(jnp.bfloat16)
    attended = jnp.einsum('kgl,kld->kgd', cache_probs.astype(jnp.float32), cache_values)
    attended = attended + jnp.einsum('kgn,nkd->kgd', fresh_probs.astype(jnp.float32), fresh_values.astype(jnp.float32))
    return attended.reshape(HEADS * HD)

def reference(x_init, queries, new_kv, kv_cache, lengths, norm_gain, w_gate_up, w_down):
    state = x_init
    block_width = D // N_TP
    results = []
    for step_index in range(STEPS):
        fresh_keys = jnp.swapaxes(new_kv[:step_index + 1, :, :, 0], 0, 1)
        fresh_values = jnp.swapaxes(new_kv[:step_index + 1, :, :, 1], 0, 1)

        def one_request(request):
            return attend_one(request[0], request[1], request[2], request[3], request[4])
        attended = lax.map(one_request, (queries[step_index], kv_cache, fresh_keys, fresh_values, lengths))
        hidden_in = state.astype(jnp.float32) + attended
        inv_rms = lax.rsqrt(lax.optimization_barrier(jnp.mean(hidden_in * hidden_in, axis=1, keepdims=True)) + 1e-05)
        normed = (hidden_in * inv_rms * norm_gain.astype(jnp.float32)).astype(jnp.bfloat16)
        gate = jnp.zeros((BATCH, FF), jnp.float32)
        up_sum = jnp.zeros((BATCH, FF), jnp.float32)
        for block_index in range(N_TP):
            lower = block_index * block_width
            feature_rows = normed[:, lower:lower + block_width]
            gate_part = jnp.dot(feature_rows, w_gate_up[lower:lower + block_width, 0], preferred_element_type=jnp.float32).astype(jnp.bfloat16)
            up_part = jnp.dot(feature_rows, w_gate_up[lower:lower + block_width, 1], preferred_element_type=jnp.float32).astype(jnp.bfloat16)
            gate_part, up_part = lax.optimization_barrier((gate_part, up_part))
            gate = gate + gate_part.astype(jnp.float32)
            up_sum = up_sum + up_part.astype(jnp.float32)
        hidden = (jax.nn.silu(gate) * up_sum).astype(jnp.bfloat16)
        down_sum = jnp.dot(hidden, w_down, preferred_element_type=jnp.float32)
        state = (hidden_in + down_sum).astype(jnp.bfloat16)
        results.append(state)
    return jnp.stack(results)
```

```python
import jax
import jax.numpy as jnp
from jax import lax
from jax.sharding import Mesh, PartitionSpec as P

D = 8192
NEAR = ("x", "zb")
FAR = ("za", "zh")
TP = ("y", "c")


def swap(array, axes):
    return lax.all_to_all(array, axes, 0, 0, tiled=True)


def spread(array, axes):
    return swap(jnp.broadcast_to(array[None], (8,) + array.shape), axes)


def attention(queries, new_kv, kv_cache, lengths):
    steps, requests, heads, size = queries.shape
    cache_length = kv_cache.shape[3]
    keys = kv_cache[:, 0, 0]
    values = kv_cache[:, 0, 1]
    rows = queries.transpose(1, 0, 2, 3).reshape(requests, steps * heads, size)
    scale = size ** (-0.5)
    scores = jnp.einsum("rqd,rld->rql", rows, keys, preferred_element_type=jnp.float32) * scale
    live = jnp.arange(cache_length, dtype=jnp.int32)[None, :] < lengths[:, None]
    scores = jnp.where(live[:, None, :], scores, -1e30)
    fresh_keys = new_kv[:, :, 0, 0]
    fresh_values = new_kv[:, :, 0, 1]
    fresh = jnp.einsum("rqd,nrd->rqn", rows, fresh_keys, preferred_element_type=jnp.float32) * scale
    row_step = jnp.arange(steps * heads, dtype=jnp.int32) // heads
    seen = jnp.arange(steps, dtype=jnp.int32)[None, :] <= row_step[:, None]
    fresh = jnp.where(seen[None], fresh, -1e30)
    top = jnp.maximum(jnp.max(scores, axis=-1), jnp.max(fresh, axis=-1))[..., None]
    cache_exp = jnp.exp(scores - top)
    fresh_exp = jnp.where(seen[None], jnp.exp(fresh - top), 0.0)
    total = jnp.sum(cache_exp, axis=-1, keepdims=True) + jnp.sum(fresh_exp, axis=-1, keepdims=True)
    cache_probs = (cache_exp / total).astype(jnp.bfloat16)
    fresh_probs = (fresh_exp / total).astype(jnp.bfloat16)
    out = jnp.einsum("rql,rld->rqd", cache_probs, values, preferred_element_type=jnp.float32)
    out = out + jnp.einsum("rqn,nrd->rqd", fresh_probs, fresh_values, preferred_element_type=jnp.float32)
    return out.reshape(requests, steps, heads * size).transpose(1, 0, 2)


def on_device(x_init, queries, new_kv, kv_cache, lengths, norm_gain, w_gate_up, w_down):
    requests, width = x_init.shape
    steps = queries.shape[0]
    units = w_gate_up.shape[2]
    w_flat = w_gate_up.reshape(width, 2 * units)
    block = 8 * requests
    with jax.named_scope("attention"):
        attended = attention(queries, new_kv, kv_cache, lengths)
    gain = norm_gain.astype(jnp.float32)
    inverse_gain = 1.0 / gain
    far_index = lax.axis_index(FAR)
    own = attended.at[0].add(x_init.astype(jnp.float32)).astype(jnp.bfloat16)
    with jax.named_scope("start_far_gather"):
        blocks = spread(own, FAR)
    blocks = blocks.astype(jnp.float32).reshape(8, steps, requests, width).transpose(1, 0, 2, 3)
    blocks = blocks.reshape(steps, block, width)
    hidden_in = blocks[0]
    results = []
    for step in range(steps):
        with jax.named_scope("near_gather"):
            rows = spread((hidden_in * gain).astype(jnp.bfloat16), NEAR).reshape(8 * block, width)
        with jax.named_scope("gate_up"):
            product = jnp.dot(rows, w_flat, preferred_element_type=jnp.float32).astype(jnp.bfloat16)
            plain = rows.astype(jnp.float32) * inverse_gain
            squares = jnp.sum(plain * plain, axis=1, keepdims=True)
            high = squares.astype(jnp.bfloat16)
            low = (squares - high.astype(jnp.float32)).astype(jnp.bfloat16)
            lane = jnp.arange(128, dtype=jnp.int32)[None, :]
            extra = jnp.where(lane == 0, high, jnp.where(lane == 1, low, jnp.zeros_like(low)))
            packed = jnp.concatenate([product, extra], axis=1).reshape(8, block, 2 * units + 128)
        with jax.named_scope("tp_scatter"):
            packed = swap(packed, TP)
        with jax.named_scope("swiglu"):
            summed = jnp.sum(packed.astype(jnp.float32), axis=0)
            mean = jnp.sum(summed[:, 2 * units :], axis=1, keepdims=True) / D
            scaled = summed[:, : 2 * units] * lax.rsqrt(mean + 1e-5)
            hidden = (jax.nn.silu(scaled[:, :units]) * scaled[:, units:]).astype(jnp.bfloat16)
        with jax.named_scope("tp_gather"):
            hidden = spread(hidden, TP).reshape(8 * block, units)
        with jax.named_scope("down"):
            down = jnp.dot(hidden, w_down, preferred_element_type=jnp.float32).astype(jnp.bfloat16)
        with jax.named_scope("near_scatter"):
            down = swap(down.reshape(8, block, width), NEAR)
        down = jnp.sum(down.astype(jnp.float32), axis=0).astype(jnp.bfloat16)
        if step + 1 < steps:
            with jax.named_scope("far_exchange"):
                down = spread(down, FAR)
            down = jnp.sum(down.astype(jnp.float32), axis=0)
            state = (hidden_in + down).astype(jnp.bfloat16)
            results.append(lax.dynamic_slice_in_dim(state, far_index * requests, requests, 0))
            hidden_in = state.astype(jnp.float32) + blocks[step + 1]
        else:
            with jax.named_scope("far_scatter"):
                down = swap(down.reshape(8, requests, width), FAR)
            down = jnp.sum(down.astype(jnp.float32), axis=0)
            mine = lax.dynamic_slice_in_dim(hidden_in, far_index * requests, requests, 0)
            results.append((mine + down).astype(jnp.bfloat16))
    return jnp.stack(results)


def solution(mesh):
    fine = Mesh(mesh.devices.reshape(4, 2, 2, 4, 4, 2), ("x", "za", "zb", "zh", "y", "c"))
    owners = ("x", "za", "zb", "zh")
    return jax.shard_map(
        on_device,
        mesh=fine,
        in_specs=(
            P(owners, TP),
            P(None, owners, TP, None),
            P(None, owners, TP, None, None),
            P(owners, TP, None, None, None),
            P(owners),
            P(TP),
            P(TP, None, owners),
            P(owners, TP),
        ),
        out_specs=P(None, owners, TP),
        check_vma=False,
    )
```

```python
import jax
import jax.numpy as jnp
from jax import lax
from jax.sharding import Mesh, PartitionSpec as P

D = 8192
NEAR = ("x", "zb")
FAR = ("za", "zh")
TP = ("y", "c")


def swap(array, axes):
    return lax.all_to_all(array, axes, 0, 0, tiled=True)


def spread(array, axes):
    return swap(jnp.broadcast_to(array[None], (8,) + array.shape), axes)


def attention(queries, new_kv, kv_cache, lengths):
    steps, requests, heads, size = queries.shape
    cache_length = kv_cache.shape[3]
    keys = kv_cache[:, 0, 0]
    values = kv_cache[:, 0, 1]
    rows = queries.transpose(1, 0, 2, 3).reshape(requests, steps * heads, size)
    scale = size ** (-0.5)
    scores = jnp.einsum("rqd,rld->rql", rows, keys, preferred_element_type=jnp.float32) * scale
    live = jnp.arange(cache_length, dtype=jnp.int32)[None, :] < lengths[:, None]
    scores = jnp.where(live[:, None, :], scores, -1e30)
    fresh_keys = new_kv[:, :, 0, 0]
    fresh_values = new_kv[:, :, 0, 1]
    fresh = jnp.einsum("rqd,nrd->rqn", rows, fresh_keys, preferred_element_type=jnp.float32) * scale
    row_step = jnp.arange(steps * heads, dtype=jnp.int32) // heads
    seen = jnp.arange(steps, dtype=jnp.int32)[None, :] <= row_step[:, None]
    fresh = jnp.where(seen[None], fresh, -1e30)
    top = jnp.maximum(jnp.max(scores, axis=-1), jnp.max(fresh, axis=-1))[..., None]
    cache_exp = jnp.exp(scores - top)
    fresh_exp = jnp.where(seen[None], jnp.exp(fresh - top), 0.0)
    total = jnp.sum(cache_exp, axis=-1, keepdims=True) + jnp.sum(fresh_exp, axis=-1, keepdims=True)
    cache_probs = (cache_exp / total).astype(jnp.bfloat16)
    fresh_probs = (fresh_exp / total).astype(jnp.bfloat16)
    out = jnp.einsum("rql,rld->rqd", cache_probs, values, preferred_element_type=jnp.float32)
    out = out + jnp.einsum("rqn,nrd->rqd", fresh_probs, fresh_values, preferred_element_type=jnp.float32)
    return out.reshape(requests, steps, heads * size).transpose(1, 0, 2)


def place_rows(mine, far_index):
    count, width = mine.shape
    row_far = jnp.arange(8, dtype=jnp.int32)[None, :, None]
    return jnp.where(row_far == far_index, mine[:, None, :], 0.0).reshape(8 * count, width)


def own_rows(rows, far_index):
    count = rows.shape[-2] // 8
    split = rows.reshape(rows.shape[:-2] + (count, 8, rows.shape[-1]))
    taken = lax.dynamic_slice_in_dim(split, far_index, 1, split.ndim - 2)
    return taken.reshape(rows.shape[:-2] + (count, rows.shape[-1]))


def on_device(x_init, queries, new_kv, kv_cache, lengths, norm_gain, w_gate_up, w_down):
    requests, width = x_init.shape
    steps = queries.shape[0]
    units = w_gate_up.shape[2]
    w_flat = w_gate_up.reshape(width, 2 * units)
    with jax.named_scope("attention"):
        attended = attention(queries, new_kv, kv_cache, lengths)
    gain = norm_gain.astype(jnp.float32)
    inverse_gain = 1.0 / gain
    far_index = lax.axis_index(FAR)
    own_first = x_init.astype(jnp.float32) + attended[0]
    with jax.named_scope("start_far_gather"):
        blocks = spread(own_first.astype(jnp.bfloat16), FAR)
    blocks, w_flat = lax.optimization_barrier((blocks, w_flat))
    blocks = blocks.astype(jnp.float32).transpose(1, 0, 2)

    def near_gather(hidden_in):
        with jax.named_scope("near_gather"):
            return spread((hidden_in * gain).astype(jnp.bfloat16), NEAR)

    def gate_up(rows):
        block = rows.shape[1]
        with jax.named_scope("gate_up"):
            product = jnp.dot(
                rows.reshape(8 * block, width), w_flat, preferred_element_type=jnp.float32
            ).astype(jnp.bfloat16)
            plain = rows.astype(jnp.float32) * inverse_gain
            squares = plain * plain
            folded = squares[..., :128]
            for lane in range(128, width, 128):
                folded = folded + squares[..., lane : lane + 128]
            packed = jnp.concatenate(
                [product.reshape(8, block, 2 * units), folded.astype(jnp.bfloat16)], axis=2
            )
        with jax.named_scope("tp_scatter"):
            return swap(packed, TP)

    def swiglu(packed):
        with jax.named_scope("swiglu"):
            summed = jnp.sum(packed.astype(jnp.float32), axis=0)
            mean = jnp.sum(summed[:, 2 * units :], axis=1, keepdims=True) / D
            scaled = summed[:, : 2 * units] * lax.rsqrt(mean + 1e-5)
            hidden = (jax.nn.silu(scaled[:, :units]) * scaled[:, units:]).astype(jnp.bfloat16)
        with jax.named_scope("tp_gather"):
            return spread(hidden, TP)

    def down_product(hidden):
        block = hidden.shape[1]
        with jax.named_scope("down"):
            down = jnp.dot(
                hidden.reshape(8 * block, units), w_down, preferred_element_type=jnp.float32
            ).astype(jnp.bfloat16)
        with jax.named_scope("near_scatter"):
            return swap(down.reshape(8, block, width), NEAR)

    def far_exchange(down, coming):
        near_sum = jnp.sum(down.astype(jnp.float32), axis=0)
        sent = (near_sum + place_rows(coming, far_index)).astype(jnp.bfloat16)
        with jax.named_scope("far_exchange"):
            return near_sum, sent, spread(sent, FAR)

    def far_scatter(down):
        near_sum = jnp.sum(down.astype(jnp.float32), axis=0).astype(jnp.bfloat16)
        count = near_sum.shape[0] // 8
        with jax.named_scope("far_scatter"):
            return swap(near_sum.reshape(count, 8, width).transpose(1, 0, 2), FAR)

    chains = ((0, 3),)
    hidden_in = [blocks[a:b].reshape((b - a) * 8, width) for a, b in chains]
    own_hidden = [own_first[a:b] for a, b in chains]
    results = []
    for step in range(steps):
        data = [near_gather(h) for h in hidden_in]
        data = [gate_up(d) for d in data]
        data = [swiglu(d) for d in data]
        data = [down_product(d) for d in data]
        if step + 1 < steps:
            coming = [attended[step + 1, a:b] for a, b in chains]
            data = [far_exchange(d, c) for d, c in zip(data, coming)]
            hidden_in = [h + jnp.sum(d[2].astype(jnp.float32), axis=0) for h, d in zip(hidden_in, data)]
            own_down = [
                jnp.sum(own_rows(got, far_index).astype(jnp.float32), axis=0)
                - own_rows(sent, far_index).astype(jnp.float32)
                + own_rows(near_sum, far_index)
                for near_sum, sent, got in data
            ]
        else:
            own_down = [jnp.sum(far_scatter(d).astype(jnp.float32), axis=0) for d in data]
        state = [(h + d).astype(jnp.bfloat16) for h, d in zip(own_hidden, own_down)]
        results.append(jnp.concatenate(state, axis=0))
        if step + 1 < steps:
            own_hidden = [s.astype(jnp.float32) + c for s, c in zip(state, coming)]
    return jnp.stack(results)


def solution(mesh):
    fine = Mesh(mesh.devices.reshape(4, 2, 2, 4, 4, 2), ("x", "za", "zb", "zh", "y", "c"))
    owners = ("x", "za", "zb", "zh")
    return jax.shard_map(
        on_device,
        mesh=fine,
        in_specs=(
            P(owners, TP),
            P(None, owners, TP, None),
            P(None, owners, TP, None, None),
            P(owners, TP, None, None, None),
            P(owners),
            P(TP),
            P(TP, None, owners),
            P(owners, TP),
        ),
        out_specs=P(None, owners, TP),
        check_vma=False,
    )
```

```python
import jax
import jax.numpy as jnp
from jax import lax
from jax.experimental import pallas as pl
from jax.experimental.pallas import tpu as pltpu
from jax.sharding import Mesh, PartitionSpec as P

D = 8192
NEAR = ("x", "zb")
FAR = ("za", "zh")
TP = ("y", "c")


def swap(array, axes):
    return lax.all_to_all(array, axes, 0, 0, tiled=True)


def spread(array, axes):
    return swap(jnp.broadcast_to(array[None], (8,) + array.shape), axes)


def attention_kernel(lengths_ref, x_ref, queries_ref, new_ref, cache_ref, out_ref, first_ref, spread_ref):
    steps, _, heads, size = queries_ref.shape
    rows = steps * heads
    scale = size ** (-0.5)
    wide = queries_ref[...].astype(jnp.float32).reshape(rows, size)
    keys = cache_ref[0, 0, 0]
    values = cache_ref[0, 0, 1]
    scores = lax.dot_general(
        wide.astype(jnp.bfloat16), keys, (((1,), (1,)), ((), ())), preferred_element_type=jnp.float32
    )
    position = lax.broadcasted_iota(jnp.int32, scores.shape, 1)
    scores = jnp.where(position < lengths_ref[pl.program_id(0)], scores * scale, -1e30)
    top = jnp.max(scores, axis=1, keepdims=True)
    row_step = lax.broadcasted_iota(jnp.int32, (rows, 1), 0) // heads
    new = new_ref[...].astype(jnp.float32)
    fresh = []
    for step in range(steps):
        score = jnp.sum(wide * new[step, 0, 0, 0:1], axis=1, keepdims=True) * scale
        fresh.append(jnp.where(row_step >= step, score, -1e30))
        top = jnp.maximum(top, fresh[-1])
    weights = jnp.exp(scores - top)
    total = jnp.sum(weights, axis=1, keepdims=True)
    for step in range(steps):
        fresh[step] = jnp.exp(fresh[step] - top)
        total = total + fresh[step]
    out = jnp.dot((weights / total).astype(jnp.bfloat16), values, preferred_element_type=jnp.float32)
    for step in range(steps):
        prob = (fresh[step] / total).astype(jnp.bfloat16).astype(jnp.float32)
        out = out + prob * new[step, 0, 0, 1:2]
    out_ref[...] = out.reshape(out_ref.shape)
    state = x_ref[...].astype(jnp.float32)
    row = lax.broadcasted_iota(jnp.int32, state.shape, 0)
    state = jnp.sum(jnp.where(row == pl.program_id(0), state, 0.0), axis=0, keepdims=True)
    state = jnp.concatenate([state[:, k * size : (k + 1) * size] for k in range(heads)], axis=0)
    first = state + out[:heads]
    first_ref[0] = first
    spread_ref[...] = jnp.broadcast_to(first.astype(jnp.bfloat16), spread_ref.shape)


def attention(x_init, queries, new_kv, kv_cache, lengths):
    steps, requests, heads, size = queries.shape
    cache_length = kv_cache.shape[3]
    out, first, spread_first = pl.pallas_call(
        attention_kernel,
        grid_spec=pltpu.PrefetchScalarGridSpec(
            num_scalar_prefetch=1,
            grid=(requests,),
            in_specs=[
                pl.BlockSpec((requests, heads * size), lambda r, _: (0, 0)),
                pl.BlockSpec((steps, 1, heads, size), lambda r, _: (0, r, 0, 0)),
                pl.BlockSpec((steps, 1, 1, 2, size), lambda r, _: (0, r, 0, 0, 0)),
                pl.BlockSpec((1, 1, 2, cache_length, size), lambda r, _: (r, 0, 0, 0, 0)),
            ],
            out_specs=[
                pl.BlockSpec((steps, 1, heads, size), lambda r, _: (0, r, 0, 0)),
                pl.BlockSpec((1, heads, size), lambda r, _: (r, 0, 0)),
                pl.BlockSpec((8, 1, heads, size), lambda r, _: (0, r, 0, 0)),
            ],
        ),
        out_shape=[
            jax.ShapeDtypeStruct((steps, requests, heads, size), jnp.float32),
            jax.ShapeDtypeStruct((requests, heads, size), jnp.float32),
            jax.ShapeDtypeStruct((8, requests, heads, size), jnp.bfloat16),
        ],
        compiler_params=pltpu.CompilerParams(vmem_limit_bytes=56 * 2**20),
    )(lengths, x_init, queries, new_kv, kv_cache)
    return (
        out.reshape(steps, requests, heads * size),
        first.reshape(requests, heads * size),
        spread_first.reshape(8, requests * heads, size),
    )


def place_rows(mine, far_index):
    count, width = mine.shape
    row_far = jnp.arange(8, dtype=jnp.int32)[None, :, None]
    return jnp.where(row_far == far_index, mine[:, None, :], 0.0).reshape(8 * count, width)


def own_rows(rows, far_index):
    count = rows.shape[-2] // 8
    split = rows.reshape(rows.shape[:-2] + (count, 8, rows.shape[-1]))
    taken = lax.dynamic_slice_in_dim(split, far_index, 1, split.ndim - 2)
    return taken.reshape(rows.shape[:-2] + (count, rows.shape[-1]))


def on_device(x_init, queries, new_kv, kv_cache, lengths, norm_gain, w_gate_up, w_down):
    requests, width = x_init.shape
    steps = queries.shape[0]
    units = w_gate_up.shape[2]
    w_flat = w_gate_up.reshape(width, 2 * units)
    with jax.named_scope("attention"):
        attended, own_first, first = attention(x_init, queries, new_kv, kv_cache, lengths)
    gain = norm_gain.astype(jnp.float32)
    inverse_gain = 1.0 / gain
    far_index = lax.axis_index(FAR)
    with jax.named_scope("start_far_gather"):
        blocks = swap(first, FAR)
    blocks, w_flat = lax.optimization_barrier((blocks, w_flat))
    blocks = blocks.reshape(8, requests, width).astype(jnp.float32).transpose(1, 0, 2)

    def near_gather(hidden_in):
        with jax.named_scope("near_gather"):
            return spread((hidden_in * gain).astype(jnp.bfloat16), NEAR)

    def gate_up(rows):
        block = rows.shape[1]
        with jax.named_scope("gate_up"):
            product = jnp.dot(
                rows.reshape(8 * block, width), w_flat, preferred_element_type=jnp.float32
            ).astype(jnp.bfloat16)
            plain = rows.astype(jnp.float32) * inverse_gain
            squares = plain * plain
            folded = squares[..., :128]
            for lane in range(128, width, 128):
                folded = folded + squares[..., lane : lane + 128]
            packed = jnp.concatenate(
                [product.reshape(8, block, 2 * units), folded.astype(jnp.bfloat16)], axis=2
            )
        with jax.named_scope("tp_scatter"):
            return swap(packed, TP)

    def swiglu(packed):
        with jax.named_scope("swiglu"):
            summed = jnp.sum(packed.astype(jnp.float32), axis=0)
            mean = jnp.sum(summed[:, 2 * units :], axis=1, keepdims=True) / D
            scaled = summed[:, : 2 * units] * lax.rsqrt(mean + 1e-5)
            hidden = (jax.nn.silu(scaled[:, :units]) * scaled[:, units:]).astype(jnp.bfloat16)
        with jax.named_scope("tp_gather"):
            return spread(hidden, TP)

    def down_product(hidden):
        block = hidden.shape[1]
        with jax.named_scope("down"):
            down = jnp.dot(
                hidden.reshape(8 * block, units), w_down, preferred_element_type=jnp.float32
            ).astype(jnp.bfloat16)
        with jax.named_scope("near_scatter"):
            return swap(down.reshape(8, block, width), NEAR)

    def far_exchange(down, coming):
        near_sum = jnp.sum(down.astype(jnp.float32), axis=0)
        sent = (near_sum + place_rows(coming, far_index)).astype(jnp.bfloat16)
        with jax.named_scope("far_exchange"):
            return near_sum, sent, spread(sent, FAR)

    def far_scatter(down):
        near_sum = jnp.sum(down.astype(jnp.float32), axis=0).astype(jnp.bfloat16)
        count = near_sum.shape[0] // 8
        with jax.named_scope("far_scatter"):
            parts = near_sum.reshape(count, 8, width).transpose(1, 0, 2)
            return swap(parts.reshape(8, 8 * count, width // 8), FAR)

    chains = ((0, 3),)
    hidden_in = [blocks[a:b].reshape((b - a) * 8, width) for a, b in chains]
    own_hidden = [own_first[a:b] for a, b in chains]
    results = []
    for step in range(steps):
        data = [near_gather(h) for h in hidden_in]
        data = [gate_up(d) for d in data]
        data = [swiglu(d) for d in data]
        data = [down_product(d) for d in data]
        if step + 1 < steps:
            coming = [attended[step + 1, a:b] for a, b in chains]
            data = [far_exchange(d, c) for d, c in zip(data, coming)]
            hidden_in = [h + jnp.sum(d[2].astype(jnp.float32), axis=0) for h, d in zip(hidden_in, data)]
            own_down = [
                jnp.sum(own_rows(got, far_index).astype(jnp.float32), axis=0)
                - own_rows(sent, far_index).astype(jnp.float32)
                + own_rows(near_sum, far_index)
                for near_sum, sent, got in data
            ]
        else:
            own_down = [
                jnp.sum(far_scatter(d).astype(jnp.float32), axis=0).reshape(h.shape)
                for d, h in zip(data, own_hidden)
            ]
        state = [(h + d).astype(jnp.bfloat16) for h, d in zip(own_hidden, own_down)]
        results.append(jnp.concatenate(state, axis=0))
        if step + 1 < steps:
            own_hidden = [s.astype(jnp.float32) + c for s, c in zip(state, coming)]
    return jnp.stack(results)


def solution(mesh):
    fine = Mesh(mesh.devices.reshape(4, 2, 2, 4, 4, 2), ("x", "za", "zb", "zh", "y", "c"))
    owners = ("x", "za", "zb", "zh")
    return jax.shard_map(
        on_device,
        mesh=fine,
        in_specs=(
            P(owners, TP),
            P(None, owners, TP, None),
            P(None, owners, TP, None, None),
            P(owners, TP, None, None, None),
            P(owners),
            P(TP),
            P(TP, None, owners),
            P(owners, TP),
        ),
        out_specs=P(None, owners, TP),
        check_vma=False,
    )
```

```python
import jax
import jax.numpy as jnp
from jax import lax
from jax.experimental import pallas as pl
from jax.experimental.pallas import tpu as pltpu
from jax.sharding import Mesh, PartitionSpec as P

D = 8192
TP = "t"


def owner(x, za, zb, zh):
    return ((x * 2 + za) * 2 + zb) * 4 + zh


def half(side, zh):
    return side ^ (zh >> 1)


NEAR = [
    [owner(x, za, half(side, zh), zh) for x in range(4) for side in range(2)]
    for za in range(2)
    for zh in range(4)
]
FAR = [
    [owner(x, za, half(side, zh), zh) for za in range(2) for zh in range(4)]
    for x in range(4)
    for side in range(2)
]


def swap(array, group):
    if group is TP:
        return lax.all_to_all(array, TP, 0, 0, tiled=True)
    return lax.all_to_all(array, "r", 0, 0, axis_index_groups=group, tiled=True)


def spread(array, axes):
    return swap(jnp.broadcast_to(array[None], (8,) + array.shape), axes)


def attention_kernel(lengths_ref, x_ref, queries_ref, new_ref, cache_ref, out_ref, first_ref, spread_ref):
    steps, _, heads, size = queries_ref.shape
    rows = steps * heads
    scale = size ** (-0.5)
    wide = queries_ref[...].astype(jnp.float32).reshape(rows, size)
    keys = cache_ref[0, 0, 0]
    values = cache_ref[0, 0, 1]
    scores = lax.dot_general(
        wide.astype(jnp.bfloat16), keys, (((1,), (1,)), ((), ())), preferred_element_type=jnp.float32
    )
    position = lax.broadcasted_iota(jnp.int32, scores.shape, 1)
    scores = jnp.where(position < lengths_ref[pl.program_id(0)], scores * scale, -1e30)
    top = jnp.max(scores, axis=1, keepdims=True)
    row_step = lax.broadcasted_iota(jnp.int32, (rows, 1), 0) // heads
    new = new_ref[...].astype(jnp.float32)
    fresh = []
    for step in range(steps):
        score = jnp.sum(wide * new[step, 0, 0, 0:1], axis=1, keepdims=True) * scale
        fresh.append(jnp.where(row_step >= step, score, -1e30))
        top = jnp.maximum(top, fresh[-1])
    weights = jnp.exp(scores - top)
    total = jnp.sum(weights, axis=1, keepdims=True)
    for step in range(steps):
        fresh[step] = jnp.exp(fresh[step] - top)
        total = total + fresh[step]
    out = jnp.dot((weights / total).astype(jnp.bfloat16), values, preferred_element_type=jnp.float32)
    for step in range(steps):
        prob = (fresh[step] / total).astype(jnp.bfloat16).astype(jnp.float32)
        out = out + prob * new[step, 0, 0, 1:2]
    out_ref[...] = out.reshape(out_ref.shape)
    state = x_ref[...].astype(jnp.float32)
    row = lax.broadcasted_iota(jnp.int32, state.shape, 0)
    state = jnp.sum(jnp.where(row == pl.program_id(0), state, 0.0), axis=0, keepdims=True)
    state = jnp.concatenate([state[:, k * size : (k + 1) * size] for k in range(heads)], axis=0)
    first = state + out[:heads]
    first_ref[0] = first
    spread_ref[...] = jnp.broadcast_to(first.astype(jnp.bfloat16), spread_ref.shape)


def attention(x_init, queries, new_kv, kv_cache, lengths):
    steps, requests, heads, size = queries.shape
    cache_length = kv_cache.shape[3]
    out, first, spread_first = pl.pallas_call(
        attention_kernel,
        grid_spec=pltpu.PrefetchScalarGridSpec(
            num_scalar_prefetch=1,
            grid=(requests,),
            in_specs=[
                pl.BlockSpec((requests, heads * size), lambda r, _: (0, 0)),
                pl.BlockSpec((steps, 1, heads, size), lambda r, _: (0, r, 0, 0)),
                pl.BlockSpec((steps, 1, 1, 2, size), lambda r, _: (0, r, 0, 0, 0)),
                pl.BlockSpec((1, 1, 2, cache_length, size), lambda r, _: (r, 0, 0, 0, 0)),
            ],
            out_specs=[
                pl.BlockSpec((steps, 1, heads, size), lambda r, _: (0, r, 0, 0)),
                pl.BlockSpec((1, heads, size), lambda r, _: (r, 0, 0)),
                pl.BlockSpec((8, 1, heads, size), lambda r, _: (0, r, 0, 0)),
            ],
        ),
        out_shape=[
            jax.ShapeDtypeStruct((steps, requests, heads, size), jnp.float32),
            jax.ShapeDtypeStruct((requests, heads, size), jnp.float32),
            jax.ShapeDtypeStruct((8, requests, heads, size), jnp.bfloat16),
        ],
        compiler_params=pltpu.CompilerParams(vmem_limit_bytes=56 * 2**20),
    )(lengths, x_init, queries, new_kv, kv_cache)
    return (
        out.reshape(steps, requests, heads * size),
        first.reshape(requests, heads * size),
        spread_first.reshape(8, requests * heads, size),
    )


def place_rows(mine, far_index):
    count, width = mine.shape
    row_far = jnp.arange(8, dtype=jnp.int32)[None, :, None]
    return jnp.where(row_far == far_index, mine[:, None, :], 0.0).reshape(8 * count, width)


def own_rows(rows, far_index):
    count = rows.shape[-2] // 8
    split = rows.reshape(rows.shape[:-2] + (count, 8, rows.shape[-1]))
    taken = lax.dynamic_slice_in_dim(split, far_index, 1, split.ndim - 2)
    return taken.reshape(rows.shape[:-2] + (count, rows.shape[-1]))


def on_device(x_init, queries, new_kv, kv_cache, lengths, norm_gain, w_gate_up, w_down):
    requests, width = x_init.shape
    steps = queries.shape[0]
    units = w_gate_up.shape[2]
    w_flat = w_gate_up.reshape(width, 2 * units)
    with jax.named_scope("attention"):
        attended, own_first, first = attention(x_init, queries, new_kv, kv_cache, lengths)
    gain = norm_gain.astype(jnp.float32)
    inverse_gain = 1.0 / gain
    place = lax.axis_index("r")
    far_index = place // 8 % 2 * 4 + place % 4
    with jax.named_scope("start_far_gather"):
        blocks = swap(first, FAR)
    placed = [place_rows(attended[step], far_index) for step in range(1, steps)]
    ready = lax.optimization_barrier((blocks, w_flat, gain, inverse_gain, placed))
    blocks, w_flat, gain, inverse_gain, placed = ready
    blocks = blocks.reshape(8, requests, width).astype(jnp.float32).transpose(1, 0, 2)
    hidden_in = blocks.reshape(requests * 8, width)

    def near_gather(hidden_in):
        with jax.named_scope("near_gather"):
            return spread((hidden_in * gain).astype(jnp.bfloat16), NEAR)

    def gate_up(rows):
        block = rows.shape[1]
        with jax.named_scope("gate_up"):
            product = jnp.dot(
                rows.reshape(8 * block, width), w_flat, preferred_element_type=jnp.float32
            ).astype(jnp.bfloat16)
            plain = rows.astype(jnp.float32) * inverse_gain
            squares = plain * plain
            folded = squares[..., :128]
            for lane in range(128, width, 128):
                folded = folded + squares[..., lane : lane + 128]
            packed = jnp.concatenate(
                [product.reshape(8, block, 2 * units), folded.astype(jnp.bfloat16)], axis=2
            )
        with jax.named_scope("tp_scatter"):
            return swap(packed, TP)

    def swiglu(packed):
        with jax.named_scope("swiglu"):
            summed = jnp.sum(packed.astype(jnp.float32), axis=0)
            mean = jnp.sum(summed[:, 2 * units :], axis=1, keepdims=True) / D
            scaled = summed[:, : 2 * units] * lax.rsqrt(mean + 1e-5)
            hidden = (jax.nn.silu(scaled[:, :units]) * scaled[:, units:]).astype(jnp.bfloat16)
        with jax.named_scope("tp_gather"):
            return spread(hidden, TP)

    def down_product(hidden):
        block = hidden.shape[1]
        with jax.named_scope("down"):
            down = jnp.dot(
                hidden.reshape(8 * block, units), w_down, preferred_element_type=jnp.float32
            ).astype(jnp.bfloat16)
        with jax.named_scope("near_scatter"):
            return swap(down.reshape(8, block, width), NEAR)

    def far_exchange(down, coming):
        near_sum = jnp.sum(down.astype(jnp.float32), axis=0)
        exact = near_sum + coming
        sent = lax.reduce_precision(exact, 8, 7)
        residual = (exact - sent).astype(jnp.bfloat16)
        with jax.named_scope("far_exchange"):
            return residual, spread(sent.astype(jnp.bfloat16), FAR)

    def far_scatter(down):
        near_sum = jnp.sum(down.astype(jnp.float32), axis=0).astype(jnp.bfloat16)
        count = near_sum.shape[0] // 8
        with jax.named_scope("far_scatter"):
            parts = near_sum.reshape(count, 8, width).transpose(1, 0, 2)
            return swap(parts.reshape(8, 8 * count, width // 8), FAR)

    exchanged = []
    for step in range(steps):
        hidden = swiglu(gate_up(near_gather(hidden_in)))
        down = down_product(hidden)
        if step + 1 < steps:
            exchanged.append(far_exchange(down, placed[step]))
            hidden_in = hidden_in + jnp.sum(exchanged[-1][1].astype(jnp.float32), axis=0)
    down, exchanged = lax.optimization_barrier((down, exchanged))
    last = far_scatter(down)
    results = []
    for step in range(steps):
        if step + 1 < steps:
            residual, got = exchanged[step]
            own_down = (
                jnp.sum(own_rows(got, far_index).astype(jnp.float32), axis=0)
                + own_rows(residual, far_index).astype(jnp.float32)
                - attended[step + 1]
            )
        else:
            own_down = jnp.sum(last.astype(jnp.float32), axis=0).reshape(own_first.shape)
        own_hidden = own_first if step == 0 else state.astype(jnp.float32) + attended[step]
        state = (own_hidden + own_down).astype(jnp.bfloat16)
        results.append(state)
    return jnp.stack(results)


def solution(mesh):
    fine = Mesh(mesh.devices.reshape(64, 8), ("r", "t"))
    owners = "r"
    return jax.shard_map(
        on_device,
        mesh=fine,
        in_specs=(
            P(owners, TP),
            P(None, owners, TP, None),
            P(None, owners, TP, None, None),
            P(owners, TP, None, None, None),
            P(owners),
            P(TP),
            P(TP, None, owners),
            P(owners, TP),
        ),
        out_specs=P(None, owners, TP),
        check_vma=False,
    )
```

```python
import jax
import jax.numpy as jnp
from jax import lax
from jax.experimental import pallas as pl
from jax.experimental.pallas import tpu as pltpu
from jax.sharding import Mesh, PartitionSpec as P

D = 8192
TP = "t"


def owner(x, za, zb, zh):
    return ((x * 2 + za) * 2 + zb) * 4 + zh


def half(side, zh):
    return side ^ (zh >> 1)


NEAR = [
    [owner(x, za, half(side, zh), zh) for side in range(2) for x in range(4)]
    for za in range(2)
    for zh in range(4)
]
FAR = [
    [owner(x, za, half(side, zh), zh) for za in range(2) for zh in range(4)]
    for x in range(4)
    for side in range(2)
]


def swap(array, group):
    if group is TP:
        return lax.all_to_all(array, TP, 0, 0, tiled=True)
    return lax.all_to_all(array, "r", 0, 0, axis_index_groups=group, tiled=True)


def spread(array, axes):
    return swap(jnp.broadcast_to(array[None], (8,) + array.shape), axes)


def attention_kernel(lengths_ref, x_ref, queries_ref, new_ref, cache_ref, out_ref, first_ref, spread_ref):
    steps, requests, heads, size = queries_ref.shape
    rows = steps * heads
    scale = size ** (-0.5)
    row_step = lax.broadcasted_iota(jnp.int32, (rows, 1), 0) // heads
    state = x_ref[...].astype(jnp.float32)
    for request in range(requests):
        wide = queries_ref[:, request].astype(jnp.float32).reshape(rows, size)
        keys = cache_ref[request, 0, 0]
        values = cache_ref[request, 0, 1]
        scores = lax.dot_general(
            wide.astype(jnp.bfloat16), keys, (((1,), (1,)), ((), ())), preferred_element_type=jnp.float32
        )
        position = lax.broadcasted_iota(jnp.int32, scores.shape, 1)
        scores = jnp.where(position < lengths_ref[request], scores * scale, -1e30)
        top = jnp.max(scores, axis=1, keepdims=True)
        new = new_ref[:, request, 0].astype(jnp.float32)
        fresh = []
        for step in range(steps):
            score = jnp.sum(wide * new[step, 0:1], axis=1, keepdims=True) * scale
            fresh.append(jnp.where(row_step >= step, score, -1e30))
            top = jnp.maximum(top, fresh[-1])
        weights = jnp.exp(scores - top)
        total = jnp.sum(weights, axis=1, keepdims=True)
        for step in range(steps):
            fresh[step] = jnp.exp(fresh[step] - top)
            total = total + fresh[step]
        out = jnp.dot((weights / total).astype(jnp.bfloat16), values, preferred_element_type=jnp.float32)
        for step in range(steps):
            prob = (fresh[step] / total).astype(jnp.bfloat16).astype(jnp.float32)
            out = out + prob * new[step, 1:2]
        out_ref[:, request] = out.reshape(steps, heads, size)
        row = state[request : request + 1]
        first = jnp.concatenate([row[:, k * size : (k + 1) * size] for k in range(heads)], axis=0)
        first = first + out[:heads]
        first_ref[request] = first
        spread_ref[:, request] = jnp.broadcast_to(first.astype(jnp.bfloat16), (8, heads, size))


def attention(x_init, queries, new_kv, kv_cache, lengths):
    steps, requests, heads, size = queries.shape
    out, first, spread_first = pl.pallas_call(
        attention_kernel,
        in_specs=[pl.BlockSpec(memory_space=pltpu.SMEM)] + [pl.BlockSpec(memory_space=pltpu.VMEM)] * 4,
        out_specs=[pl.BlockSpec(memory_space=pltpu.VMEM)] * 3,
        out_shape=[
            jax.ShapeDtypeStruct((steps, requests, heads, size), jnp.float32),
            jax.ShapeDtypeStruct((requests, heads, size), jnp.float32),
            jax.ShapeDtypeStruct((8, requests, heads, size), jnp.bfloat16),
        ],
        compiler_params=pltpu.CompilerParams(vmem_limit_bytes=56 * 2**20),
    )(lengths, x_init, queries, new_kv, kv_cache)
    return (
        out.reshape(steps, requests, heads * size),
        first.reshape(requests, heads * size),
        spread_first.reshape(8, requests * heads, size),
    )


def place_rows(mine, far_index):
    count, width = mine.shape
    row_far = jnp.arange(8, dtype=jnp.int32)[None, :, None]
    return jnp.where(row_far == far_index, mine[:, None, :], 0.0).reshape(8 * count, width)


def own_rows(rows, far_index):
    count = rows.shape[-2] // 8
    split = rows.reshape(rows.shape[:-2] + (count, 8, rows.shape[-1]))
    taken = lax.dynamic_slice_in_dim(split, far_index, 1, split.ndim - 2)
    return taken.reshape(rows.shape[:-2] + (count, rows.shape[-1]))


def on_device(x_init, queries, new_kv, kv_cache, lengths, norm_gain, w_gate_up, w_down):
    requests, width = x_init.shape
    steps = queries.shape[0]
    units = w_gate_up.shape[2]
    w_flat = w_gate_up.reshape(width, 2 * units)
    with jax.named_scope("attention"):
        attended, own_first, first = attention(x_init, queries, new_kv, kv_cache, lengths)
    gain = norm_gain.astype(jnp.float32)
    inverse_gain = 1.0 / gain
    place = lax.axis_index("r")
    far_index = place // 8 % 2 * 4 + place % 4
    with jax.named_scope("start_far_gather"):
        blocks = swap(first, FAR)
    placed = [place_rows(attended[step], far_index) for step in range(1, steps)]
    ready = lax.optimization_barrier((blocks, w_flat, gain, inverse_gain, placed))
    blocks, w_flat, gain, inverse_gain, placed = ready
    blocks = blocks.reshape(8, requests, width).astype(jnp.float32).transpose(1, 0, 2)
    hidden_in = blocks.reshape(requests * 8, width)

    def near_gather(hidden_in):
        with jax.named_scope("near_gather"):
            return spread((hidden_in * gain).astype(jnp.bfloat16), NEAR)

    def gate_up(rows):
        block = rows.shape[1]
        with jax.named_scope("gate_up"):
            product = jnp.dot(
                rows.reshape(8 * block, width), w_flat, preferred_element_type=jnp.float32
            ).astype(jnp.bfloat16)
            plain = rows.astype(jnp.float32) * inverse_gain
            squares = plain * plain
            folded = squares[..., :128]
            for lane in range(128, width, 128):
                folded = folded + squares[..., lane : lane + 128]
            packed = jnp.concatenate(
                [product.reshape(8, block, 2 * units), folded.astype(jnp.bfloat16)], axis=2
            )
        with jax.named_scope("tp_scatter"):
            return swap(packed, TP)

    def swiglu(packed):
        with jax.named_scope("swiglu"):
            summed = jnp.sum(packed.astype(jnp.float32), axis=0)
            mean = jnp.sum(summed[:, 2 * units :], axis=1, keepdims=True) / D
            scaled = summed[:, : 2 * units] * lax.rsqrt(mean + 1e-5)
            hidden = (jax.nn.silu(scaled[:, :units]) * scaled[:, units:]).astype(jnp.bfloat16)
        with jax.named_scope("tp_gather"):
            return spread(hidden, TP)

    def down_product(hidden):
        block = hidden.shape[1]
        with jax.named_scope("down"):
            down = jnp.dot(
                hidden.reshape(8 * block, units), w_down, preferred_element_type=jnp.float32
            ).astype(jnp.bfloat16)
        with jax.named_scope("near_scatter"):
            return swap(down.reshape(8, block, width), NEAR)

    def far_exchange(down, coming):
        near_sum = jnp.sum(down.astype(jnp.float32), axis=0)
        exact = near_sum + coming
        sent = lax.reduce_precision(exact, 8, 7)
        residual = (exact - sent).astype(jnp.bfloat16)
        with jax.named_scope("far_exchange"):
            return residual, spread(sent.astype(jnp.bfloat16), FAR)

    def far_scatter(down):
        near_sum = jnp.sum(down.astype(jnp.float32), axis=0).astype(jnp.bfloat16)
        count = near_sum.shape[0] // 8
        with jax.named_scope("far_scatter"):
            parts = near_sum.reshape(count, 8, width).transpose(1, 0, 2)
            return swap(parts.reshape(8, 8 * count, width // 8), FAR)

    exchanged = []
    for step in range(steps):
        hidden = swiglu(gate_up(near_gather(hidden_in)))
        down = down_product(hidden)
        if step + 1 < steps:
            exchanged.append(far_exchange(down, placed[step]))
            hidden_in = hidden_in + jnp.sum(exchanged[-1][1].astype(jnp.float32), axis=0)
    down, exchanged = lax.optimization_barrier((down, exchanged))
    last = far_scatter(down)
    results = []
    for step in range(steps):
        if step + 1 < steps:
            residual, got = exchanged[step]
            own_down = (
                jnp.sum(own_rows(got, far_index).astype(jnp.float32), axis=0)
                + own_rows(residual, far_index).astype(jnp.float32)
                - attended[step + 1]
            )
        else:
            own_down = jnp.sum(last.astype(jnp.float32), axis=0).reshape(own_first.shape)
        own_hidden = own_first if step == 0 else state.astype(jnp.float32) + attended[step]
        state = (own_hidden + own_down).astype(jnp.bfloat16)
        results.append(state)
    return jnp.stack(results)


def solution(mesh):
    fine = Mesh(mesh.devices.reshape(64, 8), ("r", "t"))
    owners = "r"
    return jax.shard_map(
        on_device,
        mesh=fine,
        in_specs=(
            P(owners, TP),
            P(None, owners, TP, None),
            P(None, owners, TP, None, None),
            P(owners, TP, None, None, None),
            P(owners),
            P(TP),
            P(TP, None, owners),
            P(owners, TP),
        ),
        out_specs=P(None, owners, TP),
        check_vma=False,
    )
```

```python
import jax
import jax.numpy as jnp
from jax import lax
from jax.experimental import pallas as pl
from jax.experimental.pallas import tpu as pltpu
from jax.sharding import Mesh, PartitionSpec as P

D = 8192
TP = "t"


def owner(x, za, zb, zh):
    return ((x * 2 + za) * 2 + zb) * 4 + zh


def half(side, zh):
    return side ^ (zh >> 1)


NEAR = [
    [owner(x, za, half(side, zh), zh) for side in range(2) for x in (0, 2, 1, 3)]
    for za in range(2)
    for zh in range(4)
]
FAR = [
    [owner(x, za, half(side, zh), zh) for za in range(2) for zh in range(4)]
    for x in range(4)
    for side in range(2)
]


def swap(array, group):
    if group is TP:
        return lax.all_to_all(array, TP, 0, 0, tiled=True)
    return lax.all_to_all(array, "r", 0, 0, axis_index_groups=group, tiled=True)


def spread(array, axes):
    return swap(jnp.broadcast_to(array[None], (8,) + array.shape), axes)


def attention_kernel(lengths_ref, x_ref, queries_ref, new_ref, cache_ref, out_ref, first_ref, spread_ref):
    steps, requests, heads, size = queries_ref.shape
    rows = steps * heads
    scale = size ** (-0.5)
    row_step = lax.broadcasted_iota(jnp.int32, (rows, 1), 0) // heads
    state = x_ref[...].astype(jnp.float32)
    for request in range(requests):
        wide = queries_ref[:, request].astype(jnp.float32).reshape(rows, size)
        keys = cache_ref[request, 0, 0]
        values = cache_ref[request, 0, 1]
        scores = lax.dot_general(
            wide.astype(jnp.bfloat16), keys, (((1,), (1,)), ((), ())), preferred_element_type=jnp.float32
        )
        position = lax.broadcasted_iota(jnp.int32, scores.shape, 1)
        scores = jnp.where(position < lengths_ref[request], scores * scale, -1e30)
        top = jnp.max(scores, axis=1, keepdims=True)
        new = new_ref[:, request, 0].astype(jnp.float32)
        fresh = []
        for step in range(steps):
            score = jnp.sum(wide * new[step, 0:1], axis=1, keepdims=True) * scale
            fresh.append(jnp.where(row_step >= step, score, -1e30))
            top = jnp.maximum(top, fresh[-1])
        weights = jnp.exp(scores - top)
        total = jnp.sum(weights, axis=1, keepdims=True)
        for step in range(steps):
            fresh[step] = jnp.exp(fresh[step] - top)
            total = total + fresh[step]
        out = jnp.dot((weights / total).astype(jnp.bfloat16), values, preferred_element_type=jnp.float32)
        for step in range(steps):
            prob = (fresh[step] / total).astype(jnp.bfloat16).astype(jnp.float32)
            out = out + prob * new[step, 1:2]
        out_ref[:, request] = out.reshape(steps, heads, size)
        row = state[request : request + 1]
        first = jnp.concatenate([row[:, k * size : (k + 1) * size] for k in range(heads)], axis=0)
        first = first + out[:heads]
        first_ref[request] = first
        spread_ref[:, request] = jnp.broadcast_to(first.astype(jnp.bfloat16), (8, heads, size))


def attention(x_init, queries, new_kv, kv_cache, lengths):
    steps, requests, heads, size = queries.shape
    out, first, spread_first = pl.pallas_call(
        attention_kernel,
        in_specs=[pl.BlockSpec(memory_space=pltpu.SMEM)] + [pl.BlockSpec(memory_space=pltpu.VMEM)] * 4,
        out_specs=[pl.BlockSpec(memory_space=pltpu.VMEM)] * 3,
        out_shape=[
            jax.ShapeDtypeStruct((steps, requests, heads, size), jnp.float32),
            jax.ShapeDtypeStruct((requests, heads, size), jnp.float32),
            jax.ShapeDtypeStruct((8, requests, heads, size), jnp.bfloat16),
        ],
        compiler_params=pltpu.CompilerParams(vmem_limit_bytes=56 * 2**20),
    )(lengths, x_init, queries, new_kv, kv_cache)
    return (
        out.reshape(steps, requests, heads * size),
        first.reshape(requests, heads * size),
        spread_first.reshape(8, requests * heads, size),
    )


def place_rows(mine, far_index):
    count, width = mine.shape
    row_far = jnp.arange(8, dtype=jnp.int32)[None, :, None]
    return jnp.where(row_far == far_index, mine[:, None, :], 0.0).reshape(8 * count, width)


def own_rows(rows, far_index):
    count = rows.shape[-2] // 8
    split = rows.reshape(rows.shape[:-2] + (count, 8, rows.shape[-1]))
    taken = lax.dynamic_slice_in_dim(split, far_index, 1, split.ndim - 2)
    return taken.reshape(rows.shape[:-2] + (count, rows.shape[-1]))


def on_device(x_init, queries, new_kv, kv_cache, lengths, norm_gain, w_gate_up, w_down):
    requests, width = x_init.shape
    steps = queries.shape[0]
    units = w_gate_up.shape[2]
    w_flat = w_gate_up.reshape(width, 2 * units)
    with jax.named_scope("attention"):
        attended, own_first, first = attention(x_init, queries, new_kv, kv_cache, lengths)
    gain = norm_gain.astype(jnp.float32)
    inverse_gain = 1.0 / gain
    place = lax.axis_index("r")
    far_index = place // 8 % 2 * 4 + place % 4
    with jax.named_scope("start_far_gather"):
        blocks = swap(first, FAR)
    placed = [place_rows(attended[step], far_index) for step in range(1, steps)]
    ready = lax.optimization_barrier((blocks, w_flat, gain, inverse_gain, placed))
    blocks, w_flat, gain, inverse_gain, placed = ready
    blocks = blocks.reshape(8, requests, width).astype(jnp.float32).transpose(1, 0, 2)
    hidden_in = blocks.reshape(requests * 8, width)

    def near_gather(hidden_in):
        with jax.named_scope("near_gather"):
            return spread((hidden_in * gain).astype(jnp.bfloat16), NEAR)

    def gate_up(rows):
        block = rows.shape[1]
        with jax.named_scope("gate_up"):
            product = jnp.dot(
                rows.reshape(8 * block, width), w_flat, preferred_element_type=jnp.float32
            ).astype(jnp.bfloat16)
            plain = rows.astype(jnp.float32) * inverse_gain
            squares = plain * plain
            folded = squares[..., :128]
            for lane in range(128, width, 128):
                folded = folded + squares[..., lane : lane + 128]
            packed = jnp.concatenate(
                [product.reshape(8, block, 2 * units), folded.astype(jnp.bfloat16)], axis=2
            )
        with jax.named_scope("tp_scatter"):
            return swap(packed, TP)

    def swiglu(packed):
        with jax.named_scope("swiglu"):
            summed = jnp.sum(packed.astype(jnp.float32), axis=0)
            mean = jnp.sum(summed[:, 2 * units :], axis=1, keepdims=True) / D
            scaled = summed[:, : 2 * units] * lax.rsqrt(mean + 1e-5)
            hidden = (jax.nn.silu(scaled[:, :units]) * scaled[:, units:]).astype(jnp.bfloat16)
        with jax.named_scope("tp_gather"):
            return spread(hidden, TP)

    def down_product(hidden):
        block = hidden.shape[1]
        with jax.named_scope("down"):
            down = jnp.dot(
                hidden.reshape(8 * block, units), w_down, preferred_element_type=jnp.float32
            ).astype(jnp.bfloat16)
        with jax.named_scope("near_scatter"):
            return swap(down.reshape(8, block, width), NEAR)

    def far_exchange(down, coming):
        near_sum = jnp.sum(down.astype(jnp.float32), axis=0)
        exact = near_sum + coming
        sent = lax.reduce_precision(exact, 8, 7)
        residual = (exact - sent).astype(jnp.bfloat16)
        with jax.named_scope("far_exchange"):
            return residual, spread(sent.astype(jnp.bfloat16), FAR)

    def far_scatter(down):
        near_sum = jnp.sum(down.astype(jnp.float32), axis=0).astype(jnp.bfloat16)
        count = near_sum.shape[0] // 8
        with jax.named_scope("far_scatter"):
            parts = near_sum.reshape(count, 8, width).transpose(1, 0, 2)
            return swap(parts.reshape(8, 8 * count, width // 8), FAR)

    exchanged = []
    for step in range(steps):
        hidden = swiglu(gate_up(near_gather(hidden_in)))
        down = down_product(hidden)
        if step + 1 < steps:
            exchanged.append(far_exchange(down, placed[step]))
            hidden_in = hidden_in + jnp.sum(exchanged[-1][1].astype(jnp.float32), axis=0)
    down, exchanged = lax.optimization_barrier((down, exchanged))
    last = far_scatter(down)
    results = []
    for step in range(steps):
        if step + 1 < steps:
            residual, got = exchanged[step]
            own_down = (
                jnp.sum(own_rows(got, far_index).astype(jnp.float32), axis=0)
                + own_rows(residual, far_index).astype(jnp.float32)
                - attended[step + 1]
            )
        else:
            own_down = jnp.sum(last.astype(jnp.float32), axis=0).reshape(own_first.shape)
        own_hidden = own_first if step == 0 else state.astype(jnp.float32) + attended[step]
        state = (own_hidden + own_down).astype(jnp.bfloat16)
        results.append(state)
    return jnp.stack(results)


def solution(mesh):
    fine = Mesh(mesh.devices.reshape(64, 8), ("r", "t"))
    owners = "r"
    return jax.shard_map(
        on_device,
        mesh=fine,
        in_specs=(
            P(owners, TP),
            P(None, owners, TP, None),
            P(None, owners, TP, None, None),
            P(owners, TP, None, None, None),
            P(owners),
            P(TP),
            P(TP, None, owners),
            P(owners, TP),
        ),
        out_specs=P(None, owners, TP),
        check_vma=False,
    )
```
